512 devices in a mesh: row: 128 (over z, y, core), col: 4 (over x).
Axes of the slice: x: 4, y: 4, z: 16, core: 2. Of those that a mesh axis runs over, the one named last changes fastest.
Arguments:
- travel_times: bfloat16 [131072, 8192], P('row', 'col'), may hold values from -18 to 18, as said below
- test_matrix: bfloat16 [8192, 512], P(('col', 'row')), may hold values from -0.198873782 to 0.198873782, as said below
Outputs:
- basis: float32 [131072, 512], P(('row', 'col'))
- factor: float32 [512, 512], P('col')
The draws below stay inside these ranges and needn't reach their ends.
Inputs may be any that keep to these rules, and one draw needn't show every extreme that they name: `travel_times`: finite values. `test_matrix`: finite values.
All inputs are finite; a program needn't handle non-finite values.
Results may differ from the reference program's by a relative error of at most 0.0003.
Values may be sent and summed in bfloat16 or wider, within the bound.
A program may use at most 64 MiB of HBM per device.

```python
import jax
import jax.numpy as jnp
from jax import lax

COLS = 8192
SKETCH = 512
ROWS_DEV = 1024
ROWS = 131072


def draw_travel_times(key, part):
    key = jax.random.fold_in(key, 11)
    first, second = jax.random.split(key, 2)
    position = jnp.arange(ROWS, dtype=jnp.float32)[:, None] / ROWS
    rough = jax.random.uniform(first, (ROWS, 1), dtype=jnp.float32)
    scales = 0.1 * jnp.power(3.0, position) * jnp.power(10.0, rough)
    noise = jnp.clip(jax.random.normal(second, (ROWS, COLS), dtype=jnp.float32), -6.0, 6.0)
    return (scales * noise).astype(jnp.bfloat16)


def draw_test_matrix(key, part):
    key = jax.random.fold_in(key, 23)
    first, second = jax.random.split(key, 2)
    column = 0.3 * jnp.power(10.0, jax.random.uniform(first, (1, SKETCH), dtype=jnp.float32))
    entries = jnp.clip(jax.random.normal(second, (COLS, SKETCH), dtype=jnp.float32), -6.0, 6.0)
    return (entries * column / jnp.sqrt(jnp.float32(COLS))).astype(jnp.bfloat16)


def setup_inputs(seed: int = 0) -> dict:
    arg_keys = jax.random.split(jax.random.key(seed), 3)
    return {
        "travel_times": draw_travel_times(jax.random.fold_in(arg_keys[2], 71), 0),
        "test_matrix": draw_test_matrix(jax.random.fold_in(arg_keys[2], 71), 0),
    }


def reference(travel_times, test_matrix):
    blocks = travel_times.reshape(ROWS // ROWS_DEV, ROWS_DEV, COLS)

    def project(block_rows):
        return jnp.dot(block_rows.astype(jnp.float32), test_matrix.astype(jnp.float32), preferred_element_type=jnp.float32)
    sketch = lax.map(project, blocks).reshape(ROWS, SKETCH)
    gram = jnp.dot(sketch.T.astype(jnp.float32), sketch.astype(jnp.float32), precision=lax.Precision.HIGHEST, preferred_element_type=jnp.float32) / ROWS
    lower_factor = jnp.linalg.cholesky(gram)
    basis = jax.scipy.linalg.solve_triangular(lower_factor, sketch.T, lower=True).T
    return (basis, lower_factor.T)
```

```python
import functools
import jax
import jax.numpy as jnp
from jax import lax
from jax.experimental import pallas as pl
from jax.experimental.pallas import tpu as pltpu
from jax.sharding import PartitionSpec as P

NY = 4
NC = 2
W = 128
CHUNKS = 4
MESH = pl.DeviceIdType.MESH


def comm_kernel(nz, nx, a_hbm, t_ref, s_ref, fin, a_v, tg, part, rsr, own, crecv, hb, prs, zr, a_sem, zs, ys, ks, rs, cs, ps, gz, ag, ck):
    ny = NY
    r = lax.axis_index("row")
    x = lax.axis_index("col")
    c = lax.rem(r, NC)
    y = lax.rem(r // NC, ny)
    z = r // (NC * ny)
    ns = ny * nx
    s = y * nx + x
    share = s_ref.shape[0]

    def row_of(zz, yy, cc):
        return (zz * ny + yy) * NC + cc

    def z_peer(i):
        return (row_of(lax.rem(z + i, nz), y, c), x)

    def plane_peer(i):
        q = lax.rem(s + i, ns)
        return q, (row_of(z, q // nx, c), lax.rem(q, nx))

    sibling = (row_of(z, y, 1 - c), x)

    load_a = pltpu.make_async_copy(a_hbm, a_v, a_sem)
    load_a.start()
    barrier = pltpu.get_barrier_semaphore()

    def greet_z(i, carry):
        pl.semaphore_signal(barrier, inc=1, device_id=z_peer(i), device_id_type=MESH)
        return carry

    def greet_plane(i, carry):
        pl.semaphore_signal(barrier, inc=1, device_id=plane_peer(i)[1], device_id_type=MESH)
        return carry

    lax.fori_loop(1, nz, greet_z, 0)
    lax.fori_loop(1, ns, greet_plane, 0)
    pl.semaphore_signal(barrier, inc=1, device_id=sibling, device_id_type=MESH)
    for j in range(CHUNKS):
        tg[j, z, y, c] = t_ref[:, j * W : (j + 1) * W]
    pl.semaphore_wait(barrier, nz + ns - 1)

    def rcopy(src, dst, sems, k, to):
        return pltpu.make_async_remote_copy(
            src_ref=src, dst_ref=dst, send_sem=sems.at[0, k], recv_sem=sems.at[1, k],
            device_id=to, device_id_type=MESH,
        )

    def wait_bytes(view, sem):
        pltpu.make_async_copy(view, view, sem).wait()

    def z_send(j):
        def body(i, carry):
            rcopy(t_ref.at[:, pl.ds(j * W, W)], tg.at[j, z, y, c], zs, j, z_peer(i)).start()
            return carry
        lax.fori_loop(1, nz, body, 0)

    def z_view(j):
        return tg.at[j, pl.ds(0, nz - 1), y, c]

    def y_send(j):
        def body(i, carry):
            rcopy(tg.at[j, :, y, c], tg.at[j, :, y, c], ys, j, (row_of(z, lax.rem(y + i, ny), c), x)).start()
            return carry
        lax.fori_loop(1, ny, body, 0)

    def y_view(j):
        return tg.at[j, :, pl.ds(0, ny - 1), c]

    def k_copy(j):
        return rcopy(tg.at[j, :, :, c], tg.at[j, :, :, c], ks, j, sibling)

    def project(j):
        t_all = tg[j].reshape(-1, W)

        def block(d):
            q = lax.rem(x + d, nx)
            rows = pl.ds(pl.multiple_of(q * share, share), share)
            return q, jnp.dot(a_v[rows, :], t_all, preferred_element_type=jnp.float32)

        def body(i, carry):
            d = nx - 1 - i
            q, value = block(d)
            part[j, d] = value
            rcopy(part.at[j, d], rsr.at[j, d - 1], rs, j, (r, q)).start()
            return carry
        lax.fori_loop(0, nx - 1, body, 0)
        part[j, 0] = block(0)[1]

    def rs_view(j):
        return rsr.at[j]

    def finish_chunk(j):
        wait_bytes(rs_view(j), rs.at[1, j])
        total = part[j, 0]
        for d in range(nx - 1):
            total = total + rsr[j, d]
        s_ref[:, j * W : (j + 1) * W] = total

    def gram_block(i, j):
        return lax.dot_general(
            s_ref[:, i * W : (i + 1) * W], s_ref[:, j * W : (j + 1) * W], (((0,), (0,)), ((), ())),
            precision=lax.Precision.HIGHEST, preferred_element_type=jnp.float32,
        )

    places = {
        0: [[(0, 0), (0, 1)], [(1, 0), (1, 1)]],
        1: [[(2, 0), (2, 1)], [(2, 2), None]],
        2: [[(3, 0), (3, 1)], [(3, 2), (3, 3)]],
    }

    def gram(g):
        for half in range(2):
            for k in range(2):
                place = places[g][half][k]
                own[g, half, :, k * W : (k + 1) * W] = jnp.zeros((W, W), jnp.float32) if place is None else gram_block(*place)
        rcopy(own.at[g, 1 - c], crecv.at[g], cs, g, sibling).start()

    def plane_send(g):
        wait_bytes(crecv.at[g], cs.at[1, g])
        hb[g] = (own[g, c] + crecv[g]).reshape(hb.shape[1:])

        def body(i, carry):
            q, to = plane_peer(i)
            rcopy(hb.at[g, q], prs.at[g, s], ps, g, to).start()
            return carry
        lax.fori_loop(1, ns, body, 0)
        prs[g, s] = hb[g, s]

    def plane_view(g):
        return prs.at[g, pl.ds(0, ns - 1)]

    def z_gram_send(g):
        wait_bytes(plane_view(g), ps.at[1, g])
        zr[g, z] = jnp.sum(prs[g], axis=0)

        def body(i, carry):
            rcopy(zr.at[g, z], zr.at[g, z], gz, g, z_peer(i)).start()
            return carry
        lax.fori_loop(1, nz, body, 0)

    def z_gram_view(g):
        return zr.at[g, pl.ds(0, nz - 1)]

    def spread(g):
        wait_bytes(z_gram_view(g), gz.at[1, g])
        fin[g, c, s] = jnp.sum(zr[g], axis=0)

        def body(i, carry):
            rcopy(fin.at[g, c, s], fin.at[g, c, s], ag, g, plane_peer(i)[1]).start()
            return carry
        lax.fori_loop(1, ns, body, 0)

    def spread_view(g):
        return fin.at[g, c, pl.ds(0, ns - 1)]

    def spread_core(g):
        wait_bytes(spread_view(g), ag.at[1, g])
        rcopy(fin.at[g, c], fin.at[g, c], ck, g, sibling).start()

    def spread_end(g):
        wait_bytes(fin.at[g, c], ck.at[1, g])

    for j in range(CHUNKS):
        z_send(j)

    def do_z(j):
        wait_bytes(z_view(j), zs.at[1, j])
        y_send(j)

    def do_y(j):
        wait_bytes(y_view(j), ys.at[1, j])
        k_copy(j).start()

    def do_k(j):
        wait_bytes(tg.at[j, :, :, c], ks.at[1, j])
        project(j)

    do_z(0)
    do_z(1)
    do_z(2)
    do_y(0)
    do_z(3)
    load_a.wait()
    do_k(0)
    do_y(1)
    do_k(1)
    do_y(2)
    do_k(2)
    do_y(3)
    do_k(3)
    finish_chunk(0)
    finish_chunk(1)
    gram(0)
    plane_send(0)
    finish_chunk(2)
    gram(1)
    plane_send(1)
    z_gram_send(0)
    finish_chunk(3)
    gram(2)
    plane_send(2)
    z_gram_send(1)
    z_gram_send(2)
    for g in range(3):
        spread(g)
        if g:
            spread_core(g - 1)
    spread_core(2)
    for g in range(3):
        spread_end(g)

    for j in range(CHUNKS):
        wait_bytes(z_view(j), zs.at[0, j])
        wait_bytes(y_view(j), ys.at[0, j])
        wait_bytes(tg.at[j, :, :, c], ks.at[0, j])
        wait_bytes(rs_view(j), rs.at[0, j])
    for g in range(3):
        wait_bytes(crecv.at[g], cs.at[0, g])
        wait_bytes(plane_view(g), ps.at[0, g])
        wait_bytes(z_gram_view(g), gz.at[0, g])
        wait_bytes(spread_view(g), ag.at[0, g])
        wait_bytes(fin.at[g, c], ck.at[0, g])


def communicate(mesh, travel_times, test_matrix):
    nx = mesh.shape["col"]
    nz = mesh.shape["row"] // (NY * NC)
    rows, cols = travel_times.shape
    depth = test_matrix.shape[0]
    share = rows // nx
    ns = NY * nx
    pr = W // ns
    f32 = jnp.float32
    dma = pltpu.SemaphoreType.DMA
    return pl.pallas_call(
        functools.partial(comm_kernel, nz, nx),
        out_shape=(
            jax.ShapeDtypeStruct((share, CHUNKS * W), f32),
            jax.ShapeDtypeStruct((3, 2, ns, pr, 2 * W), f32),
        ),
        in_specs=[pl.BlockSpec(memory_space=pl.ANY), pl.BlockSpec(memory_space=pltpu.VMEM)],
        out_specs=[pl.BlockSpec(memory_space=pltpu.VMEM)] * 2,
        scratch_shapes=[
            pltpu.VMEM((rows, cols), jnp.bfloat16),
            pltpu.VMEM((CHUNKS, nz, NY, NC, depth, W), jnp.bfloat16),
            pltpu.VMEM((CHUNKS, nx, share, W), f32),
            pltpu.VMEM((CHUNKS, nx - 1, share, W), f32),
            pltpu.VMEM((3, 2, W, 2 * W), f32),
            pltpu.VMEM((3, W, 2 * W), f32),
            pltpu.VMEM((3, ns, pr, 2 * W), f32),
            pltpu.VMEM((3, ns, pr, 2 * W), f32),
            pltpu.VMEM((3, nz, pr, 2 * W), f32),
            dma,
        ]
        + [dma((2, CHUNKS))] * 4
        + [dma((2, 3))] * 5,
        compiler_params=pltpu.CompilerParams(
            collective_id=0, has_side_effects=True, vmem_limit_bytes=40 << 20
        ),
    )(travel_times, test_matrix)


def gram_of(fin):
    halves = fin.reshape(3, 2, W, 2 * W)
    zero = jnp.zeros((W, W), jnp.float32)
    low = jnp.concatenate([
        jnp.concatenate([halves[0, 0], zero, zero], 1),
        jnp.concatenate([halves[0, 1], zero, zero], 1),
        jnp.concatenate([halves[1, 0], halves[1, 1]], 1),
        jnp.concatenate([halves[2, 0], halves[2, 1]], 1),
    ], 0)
    return low


def solution(mesh):
    def on_device(travel_times, test_matrix):
        sketch, fin = communicate(mesh, travel_times, test_matrix)
        total_rows = travel_times.shape[0] * mesh.shape["row"]
        gram_mean = gram_of(fin) / total_rows
        lower = lax.linalg.cholesky(gram_mean, symmetrize_input=False)
        basis = jax.scipy.linalg.solve_triangular(lower, sketch.T, lower=True).T
        width = lower.shape[0] // mesh.shape["col"]
        rows = lax.dynamic_slice_in_dim(lower.T, lax.axis_index("col") * width, width, 0)
        return basis, rows

    return jax.shard_map(
        on_device, mesh=mesh, in_specs=(P("row", "col"), P(("col", "row"), None)),
        out_specs=(P(("row", "col"), None), P("col", None)), check_vma=False,
    )
```

```python
import functools
import jax
import jax.numpy as jnp
from jax import lax
from jax.experimental import pallas as pl
from jax.experimental.pallas import tpu as pltpu
from jax.sharding import PartitionSpec as P

NY = 4
NC = 2
W = 128
CHUNKS = 4
MESH = pl.DeviceIdType.MESH


def comm_kernel(nz, nx, a_hbm, t_ref, s_ref, fin, a_v, tg, part, rsr, own, crecv, hb, prs, zr, a_sem, zs, ys, ks, rs, cs, ps, gz, ag, ck):
    ny = NY
    r = lax.axis_index("row")
    x = lax.axis_index("col")
    c = lax.rem(r, NC)
    y = lax.rem(r // NC, ny)
    z = r // (NC * ny)
    ns = ny * nx
    s = y * nx + x
    share = s_ref.shape[0]

    def row_of(zz, yy, cc):
        return (zz * ny + yy) * NC + cc

    def z_peer(i):
        return (row_of(lax.rem(z + i, nz), y, c), x)

    def plane_peer(i):
        q = lax.rem(s + i, ns)
        return q, (row_of(z, q // nx, c), lax.rem(q, nx))

    sibling = (row_of(z, y, 1 - c), x)

    load_a = pltpu.make_async_copy(a_hbm, a_v, a_sem)
    load_a.start()
    barrier = pltpu.get_barrier_semaphore()

    def greet_z(i, carry):
        pl.semaphore_signal(barrier, inc=1, device_id=z_peer(i), device_id_type=MESH)
        return carry

    def greet_plane(i, carry):
        pl.semaphore_signal(barrier, inc=1, device_id=plane_peer(i)[1], device_id_type=MESH)
        return carry

    lax.fori_loop(1, nz, greet_z, 0)
    lax.fori_loop(1, ns, greet_plane, 0)
    pl.semaphore_signal(barrier, inc=1, device_id=sibling, device_id_type=MESH)
    for j in range(CHUNKS):
        tg[j, z, y, c] = t_ref[:, j * W : (j + 1) * W]
    pl.semaphore_wait(barrier, nz + ns - 1)

    def rcopy(src, dst, sems, k, to):
        return pltpu.make_async_remote_copy(
            src_ref=src, dst_ref=dst, send_sem=sems.at[0, k], recv_sem=sems.at[1, k],
            device_id=to, device_id_type=MESH,
        )

    def wait_bytes(view, sem):
        pltpu.make_async_copy(view, view, sem).wait()

    def z_send(j):
        def body(i, carry):
            rcopy(t_ref.at[:, pl.ds(j * W, W)], tg.at[j, z, y, c], zs, j, z_peer(i)).start()
            return carry
        lax.fori_loop(1, nz, body, 0)

    def z_view(j):
        return tg.at[j, pl.ds(0, nz - 1), y, c]

    def y_send(j):
        def body(i, carry):
            rcopy(tg.at[j, :, y, c], tg.at[j, :, y, c], ys, j, (row_of(z, lax.rem(y + i, ny), c), x)).start()
            return carry
        lax.fori_loop(1, ny, body, 0)

    def y_view(j):
        return tg.at[j, :, pl.ds(0, ny - 1), c]

    def k_copy(j):
        return rcopy(tg.at[j, :, :, c], tg.at[j, :, :, c], ks, j, sibling)

    def project(j):
        t_all = tg[j].reshape(-1, W)

        def block(d):
            q = lax.rem(x + d, nx)
            rows = pl.ds(pl.multiple_of(q * share, share), share)
            return q, jnp.dot(a_v[rows, :], t_all, preferred_element_type=jnp.float32)

        def body(i, carry):
            d = nx - 1 - i
            q, value = block(d)
            part[j, d] = value
            rcopy(part.at[j, d], rsr.at[j, d - 1], rs, j, (r, q)).start()
            return carry
        lax.fori_loop(0, nx - 1, body, 0)
        part[j, 0] = block(0)[1]

    def rs_view(j):
        return rsr.at[j]

    def finish_chunk(j):
        wait_bytes(rs_view(j), rs.at[1, j])
        total = part[j, 0]
        for d in range(nx - 1):
            total = total + rsr[j, d]
        s_ref[:, j * W : (j + 1) * W] = total

    def gram_block(i, j):
        return lax.dot_general(
            s_ref[:, i * W : (i + 1) * W], s_ref[:, j * W : (j + 1) * W], (((0,), (0,)), ((), ())),
            precision=lax.Precision.HIGHEST, preferred_element_type=jnp.float32,
        )

    places = {
        0: [[(0, 0), (0, 1)], [(1, 0), (1, 1)]],
        1: [[(2, 0), (2, 1)], [(2, 2), None]],
        2: [[(3, 0), (3, 1)], [(3, 2), (3, 3)]],
    }

    def gram(g):
        for half in range(2):
            for k in range(2):
                place = places[g][half][k]
                own[g, half, :, k * W : (k + 1) * W] = jnp.zeros((W, W), jnp.float32) if place is None else gram_block(*place)
        rcopy(own.at[g, 1 - c], crecv.at[g], cs, g, sibling).start()

    def plane_send(g):
        wait_bytes(crecv.at[g], cs.at[1, g])
        hb[g] = (own[g, c] + crecv[g]).reshape(hb.shape[1:])

        def body(i, carry):
            q, to = plane_peer(i)
            rcopy(hb.at[g, q], prs.at[g, s], ps, g, to).start()
            return carry
        lax.fori_loop(1, ns, body, 0)
        prs[g, s] = hb[g, s]

    def plane_view(g):
        return prs.at[g, pl.ds(0, ns - 1)]

    def z_gram_send(g):
        wait_bytes(plane_view(g), ps.at[1, g])
        zr[g, z] = jnp.sum(prs[g], axis=0)

        def body(i, carry):
            rcopy(zr.at[g, z], zr.at[g, z], gz, g, z_peer(i)).start()
            return carry
        lax.fori_loop(1, nz, body, 0)

    def z_gram_view(g):
        return zr.at[g, pl.ds(0, nz - 1)]

    def spread(g):
        wait_bytes(z_gram_view(g), gz.at[1, g])
        fin[g, c, s] = jnp.sum(zr[g], axis=0)

        def body(i, carry):
            rcopy(fin.at[g, c, s], fin.at[g, c, s], ag, g, plane_peer(i)[1]).start()
            return carry
        lax.fori_loop(1, ns, body, 0)

    def spread_view(g):
        return fin.at[g, c, pl.ds(0, ns - 1)]

    def spread_core(g):
        wait_bytes(spread_view(g), ag.at[1, g])
        rcopy(fin.at[g, c], fin.at[g, c], ck, g, sibling).start()

    def spread_end(g):
        wait_bytes(fin.at[g, c], ck.at[1, g])

    for j in range(CHUNKS):
        z_send(j)

    def do_z(j):
        wait_bytes(z_view(j), zs.at[1, j])
        y_send(j)

    def do_y(j):
        wait_bytes(y_view(j), ys.at[1, j])
        k_copy(j).start()

    def do_k(j):
        wait_bytes(tg.at[j, :, :, c], ks.at[1, j])
        project(j)

    do_z(0)
    do_z(1)
    do_z(2)
    do_y(0)
    do_z(3)
    load_a.wait()
    do_k(0)
    do_y(1)
    do_k(1)
    do_y(2)
    do_k(2)
    do_y(3)
    do_k(3)
    finish_chunk(0)
    finish_chunk(1)
    gram(0)
    plane_send(0)
    finish_chunk(2)
    gram(1)
    plane_send(1)
    z_gram_send(0)
    finish_chunk(3)
    gram(2)
    plane_send(2)
    z_gram_send(1)
    z_gram_send(2)
    for g in range(3):
        spread(g)
        if g:
            spread_core(g - 1)
    spread_core(2)
    for g in range(3):
        spread_end(g)

    for j in range(CHUNKS):
        wait_bytes(z_view(j), zs.at[0, j])
        wait_bytes(y_view(j), ys.at[0, j])
        wait_bytes(tg.at[j, :, :, c], ks.at[0, j])
        wait_bytes(rs_view(j), rs.at[0, j])
    for g in range(3):
        wait_bytes(crecv.at[g], cs.at[0, g])
        wait_bytes(plane_view(g), ps.at[0, g])
        wait_bytes(z_gram_view(g), gz.at[0, g])
        wait_bytes(spread_view(g), ag.at[0, g])
        wait_bytes(fin.at[g, c], ck.at[0, g])


def communicate(mesh, travel_times, test_matrix):
    nx = mesh.shape["col"]
    nz = mesh.shape["row"] // (NY * NC)
    rows, cols = travel_times.shape
    depth = test_matrix.shape[0]
    share = rows // nx
    ns = NY * nx
    pr = W // ns
    f32 = jnp.float32
    dma = pltpu.SemaphoreType.DMA
    return pl.pallas_call(
        functools.partial(comm_kernel, nz, nx),
        out_shape=(
            jax.ShapeDtypeStruct((share, CHUNKS * W), f32),
            jax.ShapeDtypeStruct((3, 2, ns, pr, 2 * W), f32),
        ),
        in_specs=[pl.BlockSpec(memory_space=pl.ANY), pl.BlockSpec(memory_space=pltpu.VMEM)],
        out_specs=[pl.BlockSpec(memory_space=pltpu.VMEM)] * 2,
        scratch_shapes=[
            pltpu.VMEM((rows, cols), jnp.bfloat16),
            pltpu.VMEM((CHUNKS, nz, NY, NC, depth, W), jnp.bfloat16),
            pltpu.VMEM((CHUNKS, nx, share, W), f32),
            pltpu.VMEM((CHUNKS, nx - 1, share, W), f32),
            pltpu.VMEM((3, 2, W, 2 * W), f32),
            pltpu.VMEM((3, W, 2 * W), f32),
            pltpu.VMEM((3, ns, pr, 2 * W), f32),
            pltpu.VMEM((3, ns, pr, 2 * W), f32),
            pltpu.VMEM((3, nz, pr, 2 * W), f32),
            dma,
        ]
        + [dma((2, CHUNKS))] * 4
        + [dma((2, 3))] * 5,
        compiler_params=pltpu.CompilerParams(
            collective_id=0, has_side_effects=True, vmem_limit_bytes=40 << 20
        ),
    )(travel_times, test_matrix)


HIGHEST = lax.Precision.HIGHEST


def mm(a, b, ca, cb):
    return lax.dot_general(a, b, (((ca,), (cb,)), ((), ())), precision=HIGHEST, preferred_element_type=jnp.float32)


def factor_block(w_ref, q_ref):
    n = W // 8
    sub = lax.broadcasted_iota(jnp.int32, (8, W), 0)
    lane = lax.broadcasted_iota(jnp.int32, (8, W), 1)

    def along(v, i):
        return jnp.broadcast_to(v[:, i : i + 1], (8, W))

    def down(v, i):
        return jnp.broadcast_to(v[i : i + 1, :], (8, W))

    for t in range(n):
        q_ref[8 * t : 8 * t + 8, :] = jnp.where(lane == sub + 8 * t, 1.0, 0.0).astype(jnp.float32)
    for k in range(n):
        p = w_ref[8 * k : 8 * k + 8, :]
        q = q_ref[8 * k : 8 * k + 8, :]
        cols = [along(p, 8 * k + m) for m in range(8)]
        rinv, below, us, qs = [], [], [], []
        for m in range(8):
            ri = lax.rsqrt(down(cols[m], m))
            l = cols[m] * ri
            pivots = {}
            for i in range(m + 1, 8):
                pivots[i] = down(l, i)
                cols[i] = cols[i] - l * pivots[i]
            lm = jnp.where(sub > m, l, 0.0)
            u = down(p, m) * ri
            v = down(q, m) * ri
            p = jnp.where(sub == m, u, p - lm * u)
            q = jnp.where(sub == m, v, q - lm * v)
            rinv.append(ri)
            below.append(pivots)
            us.append(u)
            qs.append(v)
        w_ref[8 * k : 8 * k + 8, :] = p
        q_ref[8 * k : 8 * k + 8, :] = q
        for t in range(k + 1, n):
            wt = w_ref[8 * t : 8 * t + 8, :]
            qt = q_ref[8 * t : 8 * t + 8, :]
            ct = [along(wt, 8 * k + m) for m in range(8)]
            for m in range(8):
                l = ct[m] * rinv[m]
                for i in range(m + 1, 8):
                    ct[i] = ct[i] - l * below[m][i]
                wt = wt - l * us[m]
                qt = qt - l * qs[m]
            w_ref[8 * t : 8 * t + 8, :] = wt
            q_ref[8 * t : 8 * t + 8, :] = qt


def factor_kernel(scale, s_ref, fin, basis_ref, out_ref, upper, low, inv, w_ref, q_ref):
    nb = CHUNKS
    row = lax.broadcasted_iota(jnp.int32, (W, W), 0)
    col = lax.broadcasted_iota(jnp.int32, (W, W), 1)

    def gram(i, j):
        if i < 2:
            g, half, k = 0, i, j
        else:
            g, half, k = i - 1, j // 2, j % 2
        return fin[g, half, :, k * W : (k + 1) * W] * scale

    upper[...] = jnp.zeros_like(upper)
    for b in range(nb):
        acc = gram(b, b)
        for m in range(b):
            acc = acc - mm(low[b, m], low[b, m], 1, 1)
        w_ref[...] = acc
        factor_block(w_ref, q_ref)
        q = q_ref[...]
        upper[b, :, b * W : (b + 1) * W] = jnp.where(col >= row, w_ref[...], 0.0)
        inv[b, b] = q
        for j in range(b + 1, nb):
            a = gram(j, b)
            for m in range(b):
                a = a - mm(low[j, m], low[b, m], 1, 1)
            a = mm(a, q, 1, 1)
            low[j, b] = a
            upper[b, :, j * W : (j + 1) * W] = a.T
        for j in range(b):
            total = mm(low[b, j], inv[j, j], 1, 0)
            for m in range(j + 1, b):
                total = total + mm(low[b, m], inv[m, j], 1, 0)
            inv[b, j] = -mm(q, total, 1, 0)
        value = mm(s_ref[:, 0:W], inv[b, 0], 1, 1)
        for m in range(1, b + 1):
            value = value + mm(s_ref[:, m * W : (m + 1) * W], inv[b, m], 1, 1)
        basis_ref[:, b * W : (b + 1) * W] = value
    out_ref[...] = upper[lax.axis_index("col")]


def finish(scale, sketch, fin):
    f32 = jnp.float32
    rows, width = sketch.shape
    return pl.pallas_call(
        functools.partial(factor_kernel, scale),
        out_shape=(jax.ShapeDtypeStruct((rows, width), f32), jax.ShapeDtypeStruct((W, width), f32)),
        in_specs=[pl.BlockSpec(memory_space=pltpu.VMEM)] * 2,
        out_specs=[pl.BlockSpec(memory_space=pltpu.VMEM)] * 2,
        scratch_shapes=[
            pltpu.VMEM((CHUNKS, W, width), f32),
            pltpu.VMEM((CHUNKS, CHUNKS, W, W), f32),
            pltpu.VMEM((CHUNKS, CHUNKS, W, W), f32),
            pltpu.VMEM((W, W), f32),
            pltpu.VMEM((W, W), f32),
        ],
        compiler_params=pltpu.CompilerParams(vmem_limit_bytes=40 << 20),
    )(sketch, fin)


def solution(mesh):
    def on_device(travel_times, test_matrix):
        sketch, fin = communicate(mesh, travel_times, test_matrix)
        total_rows = travel_times.shape[0] * mesh.shape["row"]
        return finish(1.0 / total_rows, sketch, fin.reshape(3, 2, W, 2 * W))

    return jax.shard_map(
        on_device, mesh=mesh, in_specs=(P("row", "col"), P(("col", "row"), None)),
        out_specs=(P(("row", "col"), None), P("col", None)), check_vma=False,
    )
```

```python
import functools
import jax
import jax.numpy as jnp
from jax import lax
from jax.experimental import pallas as pl
from jax.experimental.pallas import tpu as pltpu
from jax.sharding import PartitionSpec as P

NY = 4
NC = 2
W = 128
CHUNKS = 4
VMEM_MIB = 40
MESH = pl.DeviceIdType.MESH


HIGHEST = lax.Precision.HIGHEST


def mm(a, b, ca, cb):
    return lax.dot_general(a, b, (((ca,), (cb,)), ((), ())), precision=HIGHEST, preferred_element_type=jnp.float32)


def factor_block(w_ref, q_ref, hooks=None):
    n = W // 8
    sub = lax.broadcasted_iota(jnp.int32, (8, W), 0)
    lane = lax.broadcasted_iota(jnp.int32, (8, W), 1)

    def along(v, i):
        return jnp.broadcast_to(v[:, i : i + 1], (8, W))

    def down(v, i):
        return jnp.broadcast_to(v[i : i + 1, :], (8, W))

    for t in range(n):
        q_ref[8 * t : 8 * t + 8, :] = jnp.where(lane == sub + 8 * t, 1.0, 0.0).astype(jnp.float32)
    for k in range(n):
        if hooks and k in hooks:
            hooks[k]()
        p = w_ref[8 * k : 8 * k + 8, :]
        q = q_ref[8 * k : 8 * k + 8, :]
        cols = [along(p, 8 * k + m) for m in range(8)]
        rinv, below, us, qs = [], [], [], []
        for m in range(8):
            ri = lax.rsqrt(down(cols[m], m))
            l = cols[m] * ri
            pivots = {}
            for i in range(m + 1, 8):
                pivots[i] = down(l, i)
                cols[i] = cols[i] - l * pivots[i]
            lm = jnp.where(sub > m, l, 0.0)
            u = down(p, m) * ri
            v = down(q, m) * ri
            p = jnp.where(sub == m, u, p - lm * u)
            q = jnp.where(sub == m, v, q - lm * v)
            rinv.append(ri)
            below.append(pivots)
            us.append(u)
            qs.append(v)
        w_ref[8 * k : 8 * k + 8, :] = p
        q_ref[8 * k : 8 * k + 8, :] = q
        for t in range(k + 1, n):
            wt = w_ref[8 * t : 8 * t + 8, :]
            qt = q_ref[8 * t : 8 * t + 8, :]
            ct = [along(wt, 8 * k + m) for m in range(8)]
            for m in range(8):
                l = ct[m] * rinv[m]
                for i in range(m + 1, 8):
                    ct[i] = ct[i] - l * below[m][i]
                wt = wt - l * us[m]
                qt = qt - l * qs[m]
            w_ref[8 * t : 8 * t + 8, :] = wt
            q_ref[8 * t : 8 * t + 8, :] = qt


def sketch_kernel(nz, nx, scale, a_hbm, t_ref, basis_ref, out_ref, a_v, tg, part, rsr, s_ref, own, crecv, hb, prs, zr, fin, left, low, upper, diag, w_ref, q_ref, a_sem, zs, ys, ks, rs, cs, ps, gz, ag, ck):
    ny = NY
    r = lax.axis_index("row")
    x = lax.axis_index("col")
    c = lax.rem(r, NC)
    y = lax.rem(r // NC, ny)
    z = r // (NC * ny)
    ns = ny * nx
    s = y * nx + x
    share = s_ref.shape[0]

    def row_of(zz, yy, cc):
        return (zz * ny + yy) * NC + cc

    def z_peer(i):
        return (row_of(lax.rem(z + i, nz), y, c), x)

    nu = 2 * ns
    zb = lax.rem(z, 2)
    zp = z // 2
    nzp = nz // 2
    u = zb * ns + s

    def pair_peer(i):
        v = lax.rem(u + i, nu)
        q = lax.rem(v, ns)
        return v, (row_of(2 * zp + v // ns, q // nx, c), lax.rem(q, nx))

    def far_peer(i):
        return (row_of(2 * lax.rem(zp + i, nzp) + zb, y, c), x)

    sibling = (row_of(z, y, 1 - c), x)

    load_a = pltpu.make_async_copy(a_hbm, a_v, a_sem)
    load_a.start()
    barrier = pltpu.get_barrier_semaphore()

    def greet_z(i, carry):
        pl.semaphore_signal(barrier, inc=1, device_id=z_peer(i), device_id_type=MESH)
        return carry

    def greet_pair(i, carry):
        pl.semaphore_signal(barrier, inc=1, device_id=pair_peer(i)[1], device_id_type=MESH)
        return carry

    lax.fori_loop(1, nz, greet_z, 0)
    lax.fori_loop(1, nu, greet_pair, 0)
    pl.semaphore_signal(barrier, inc=1, device_id=sibling, device_id_type=MESH)
    for j in range(CHUNKS):
        tg[j, z, y, c] = t_ref[:, j * W : (j + 1) * W]
    pl.semaphore_wait(barrier, nz + nu - 1)

    def rcopy(src, dst, sems, k, to):
        return pltpu.make_async_remote_copy(
            src_ref=src, dst_ref=dst, send_sem=sems.at[0, k], recv_sem=sems.at[1, k],
            device_id=to, device_id_type=MESH,
        )

    def wait_bytes(view, sem):
        pltpu.make_async_copy(view, view, sem).wait()

    def z_send(j):
        def body(i, carry):
            rcopy(t_ref.at[:, pl.ds(j * W, W)], tg.at[j, z, y, c], zs, j, z_peer(i)).start()
            return carry
        lax.fori_loop(1, nz, body, 0)

    def z_view(j):
        return tg.at[j, pl.ds(0, nz - 1), y, c]

    def y_send(j):
        def body(i, carry):
            rcopy(tg.at[j, :, y, c], tg.at[j, :, y, c], ys, j, (row_of(z, lax.rem(y + i, ny), c), x)).start()
            return carry
        lax.fori_loop(1, ny, body, 0)

    def y_view(j):
        return tg.at[j, :, pl.ds(0, ny - 1), c]

    def k_copy(j):
        return rcopy(tg.at[j, :, :, c], tg.at[j, :, :, c], ks, j, sibling)

    def project(j):
        t_all = tg[j].reshape(-1, W)

        def block(d):
            q = lax.rem(x + d, nx)
            rows = pl.ds(pl.multiple_of(q * share, share), share)
            return q, jnp.dot(a_v[rows, :], t_all, preferred_element_type=jnp.float32)

        def body(i, carry):
            d = nx - 1 - i
            q, value = block(d)
            part[j, d] = value
            rcopy(part.at[j, d], rsr.at[j, d - 1], rs, j, (r, q)).start()
            return carry
        lax.fori_loop(0, nx - 1, body, 0)
        part[j, 0] = block(0)[1]

    def rs_view(j):
        return rsr.at[j]

    def finish_chunk(j):
        wait_bytes(rs_view(j), rs.at[1, j])
        total = part[j, 0]
        for d in range(nx - 1):
            total = total + rsr[j, d]
        s_ref[:, j * W : (j + 1) * W] = total

    def gram_block(i, j):
        return lax.dot_general(
            s_ref[:, i * W : (i + 1) * W], s_ref[:, j * W : (j + 1) * W], (((0,), (0,)), ((), ())),
            precision=lax.Precision.HIGHEST, preferred_element_type=jnp.float32,
        )

    places = {
        0: [[(0, 0), (0, 1)], [(1, 0), (1, 1)]],
        1: [[(2, 0), (2, 1)], [(2, 2), None]],
        2: [[(3, 0), (3, 1)], [(3, 2), (3, 3)]],
    }

    def gram(g):
        for half in range(2):
            for k in range(2):
                place = places[g][half][k]
                own[g, half, k] = jnp.zeros((W, W), jnp.float32) if place is None else gram_block(*place)
        rcopy(own.at[g, 1 - c], crecv.at[g], cs, g, sibling).start()

    def pair_send(g):
        wait_bytes(crecv.at[g], cs.at[1, g])
        hb[g] = (own[g, c] + crecv[g]).reshape(hb.shape[1:])

        def body(i, carry):
            v, to = pair_peer(i)
            rcopy(hb.at[g, v], prs.at[g, u], ps, g, to).start()
            return carry
        lax.fori_loop(1, nu, body, 0)
        prs[g, u] = hb[g, u]

    def pair_view(g):
        return prs.at[g, pl.ds(0, nu - 1)]

    def far_send(g):
        wait_bytes(pair_view(g), ps.at[1, g])
        zr[g, zp] = jnp.sum(prs[g], axis=0)

        def body(i, carry):
            rcopy(zr.at[g, zp], zr.at[g, zp], gz, g, far_peer(i)).start()
            return carry
        lax.fori_loop(1, nzp, body, 0)

    def far_view(g):
        return zr.at[g, pl.ds(0, nzp - 1)]

    def spread(g):
        wait_bytes(far_view(g), gz.at[1, g])
        fin[g, c, u] = jnp.sum(zr[g], axis=0)

        def body(i, carry):
            rcopy(fin.at[g, c, u], fin.at[g, c, u], ag, g, pair_peer(i)[1]).start()
            return carry
        lax.fori_loop(1, nu, body, 0)

    def spread_view(g):
        return fin.at[g, c, pl.ds(0, nu - 1)]

    def spread_core(g):
        wait_bytes(spread_view(g), ag.at[1, g])
        rcopy(fin.at[g, c], fin.at[g, c], ck, g, sibling).start()

    def spread_end(g):
        wait_bytes(fin.at[g, c], ck.at[1, g])

    row_at = lax.broadcasted_iota(jnp.int32, (W, W), 0)
    col_at = lax.broadcasted_iota(jnp.int32, (W, W), 1)
    done = []
    arrived = []

    def catch_up(j, b):
        l = mm(left[j, b], diag[b], 1, 1)
        low[j, b] = l
        for i in range(b + 1, j + 1):
            left[j, i] = left[j, i] - mm(l, low[i, b], 1, 1)

    def settle(j, b):
        l = low[j, b]
        upper[b, :, j * W : (j + 1) * W] = l.T
        block = (slice(None), slice(j * W, (j + 1) * W))
        basis_ref[block] = basis_ref[block] - mm(basis_ref[:, b * W : (b + 1) * W], l, 1, 1)

    def arrive(j):
        if j < 2:
            g, half = 0, j
        else:
            g = j - 1
        for i in range(j + 1):
            f, k = (half, i) if j < 2 else (i // 2, i % 2)
            left[j, i] = fin[g, f, k * ns : (k + 1) * ns].reshape(W, W) * scale
        basis_ref[:, j * W : (j + 1) * W] = s_ref[:, j * W : (j + 1) * W]
        arrived.append(j)
        for b in done:
            catch_up(j, b)
        for b in done:
            settle(j, b)

    def factor(b, hooks=None):
        w_ref[...] = left[b, b]
        factor_block(w_ref, q_ref, hooks)
        q = q_ref[...]
        diag[b] = q
        upper[b, :, b * W : (b + 1) * W] = jnp.where(col_at >= row_at, w_ref[...], 0.0)
        later = [j for j in arrived if j > b]
        for j in later:
            catch_up(j, b)
        block = (slice(None), slice(b * W, (b + 1) * W))
        basis_ref[block] = mm(basis_ref[block], q, 1, 1)
        for j in later:
            settle(j, b)
        done.append(b)

    for j in range(CHUNKS):
        z_send(j)

    def do_z(j):
        wait_bytes(z_view(j), zs.at[1, j])
        y_send(j)

    def do_y(j):
        wait_bytes(y_view(j), ys.at[1, j])
        k_copy(j).start()

    def do_k(j):
        wait_bytes(tg.at[j, :, :, c], ks.at[1, j])
        project(j)

    do_z(0)
    do_z(1)
    do_z(2)
    do_y(0)
    do_z(3)
    load_a.wait()
    do_k(0)
    do_y(1)
    do_k(1)
    do_y(2)
    do_k(2)
    do_y(3)
    do_k(3)
    finish_chunk(0)
    finish_chunk(1)
    gram(0)
    pair_send(0)
    finish_chunk(2)
    gram(1)
    pair_send(1)
    far_send(0)
    finish_chunk(3)
    gram(2)
    pair_send(2)
    far_send(1)
    spread(0)
    far_send(2)
    upper[...] = jnp.zeros_like(upper)
    spread(1)
    spread_core(0)
    spread_end(0)
    arrive(0)
    arrive(1)
    factor(0)
    spread(2)
    spread_core(1)
    factor(1)
    spread_end(1)
    arrive(2)

    def last_group():
        spread_core(2)

    factor(2, {8: last_group})
    spread_end(2)
    arrive(3)
    factor(3)
    out_ref[...] = upper[x]

    for j in range(CHUNKS):
        wait_bytes(z_view(j), zs.at[0, j])
        wait_bytes(y_view(j), ys.at[0, j])
        wait_bytes(tg.at[j, :, :, c], ks.at[0, j])
        wait_bytes(rs_view(j), rs.at[0, j])
    for g in range(3):
        wait_bytes(crecv.at[g], cs.at[0, g])
        wait_bytes(pair_view(g), ps.at[0, g])
        wait_bytes(far_view(g), gz.at[0, g])
        wait_bytes(spread_view(g), ag.at[0, g])
        wait_bytes(fin.at[g, c], ck.at[0, g])


def solution(mesh):
    nx = mesh.shape["col"]
    nz = mesh.shape["row"] // (NY * NC)
    ns = NY * nx
    pr = W // ns
    f32 = jnp.float32
    dma = pltpu.SemaphoreType.DMA

    def on_device(travel_times, test_matrix):
        rows, cols = travel_times.shape
        depth, width = test_matrix.shape
        share = rows // nx
        scale = 1.0 / (rows * mesh.shape["row"])
        return pl.pallas_call(
            functools.partial(sketch_kernel, nz, nx, scale),
            out_shape=(
                jax.ShapeDtypeStruct((share, width), f32),
                jax.ShapeDtypeStruct((width // nx, width), f32),
            ),
            in_specs=[pl.BlockSpec(memory_space=pl.ANY), pl.BlockSpec(memory_space=pltpu.VMEM)],
            out_specs=[pl.BlockSpec(memory_space=pltpu.VMEM)] * 2,
            scratch_shapes=[
                pltpu.VMEM((rows, cols), jnp.bfloat16),
                pltpu.VMEM((CHUNKS, nz, NY, NC, depth, W), jnp.bfloat16),
                pltpu.VMEM((CHUNKS, nx, share, W), f32),
                pltpu.VMEM((CHUNKS, nx - 1, share, W), f32),
                pltpu.VMEM((share, width), f32),
                pltpu.VMEM((3, 2, 2, W, W), f32),
                pltpu.VMEM((3, 2, W, W), f32),
                pltpu.VMEM((3, 2 * ns, pr, W), f32),
                pltpu.VMEM((3, 2 * ns, pr, W), f32),
                pltpu.VMEM((3, nz // 2, pr, W), f32),
                pltpu.VMEM((3, 2, 2 * ns, pr, W), f32),
                pltpu.VMEM((CHUNKS, CHUNKS, W, W), f32),
                pltpu.VMEM((CHUNKS, CHUNKS, W, W), f32),
                pltpu.VMEM((CHUNKS, W, width), f32),
                pltpu.VMEM((CHUNKS, W, W), f32),
                pltpu.VMEM((W, W), f32),
                pltpu.VMEM((W, W), f32),
                dma,
            ]
            + [dma((2, CHUNKS))] * 4
            + [dma((2, 3))] * 5,
            compiler_params=pltpu.CompilerParams(
                collective_id=0, has_side_effects=True, vmem_limit_bytes=VMEM_MIB << 20
            ),
        )(travel_times, test_matrix)

    return jax.shard_map(
        on_device, mesh=mesh, in_specs=(P("row", "col"), P(("col", "row"), None)),
        out_specs=(P(("row", "col"), None), P("col", None)), check_vma=False,
    )
```

```python
import functools
import jax
import jax.numpy as jnp
from jax import lax
from jax.experimental import pallas as pl
from jax.experimental.pallas import tpu as pltpu
from jax.sharding import PartitionSpec as P

NY = 4
NC = 2
W = 128
CHUNKS = 4
VMEM_MIB = 58
MESH = pl.DeviceIdType.MESH


HIGHEST = lax.Precision.HIGHEST


def mm(a, b, ca, cb):
    return lax.dot_general(a, b, (((ca,), (cb,)), ((), ())), precision=HIGHEST, preferred_element_type=jnp.float32)


def factor_block(w_ref, q_ref, hooks=None):
    n = W // 8
    sub = lax.broadcasted_iota(jnp.int32, (8, W), 0)
    lane = lax.broadcasted_iota(jnp.int32, (8, W), 1)

    def along(v, i):
        return jnp.broadcast_to(v[:, i : i + 1], (8, W))

    def down(v, i):
        return jnp.broadcast_to(v[i : i + 1, :], (8, W))

    for t in range(n):
        q_ref[8 * t : 8 * t + 8, :] = jnp.where(lane == sub + 8 * t, 1.0, 0.0).astype(jnp.float32)
    first = w_ref[0:8, :]
    cols = [along(first, m) for m in range(8)]
    for k in range(n):
        if hooks and k in hooks:
            hooks[k]()
        here = slice(8 * k, 8 * k + 8)
        after = slice(8 * k + 8, 8 * k + 16)
        p = w_ref[here, :]
        q = q_ref[here, :]
        more = k + 1 < n
        if more:
            wn = w_ref[after, :]
            qn = q_ref[after, :]
            cn = [along(wn, 8 * k + m) for m in range(8)]
            dn = [along(wn, 8 * k + 8 + m) for m in range(8)]
        rinv, below, us, qs = [], [], [], []
        for m in range(8):
            ri = lax.rsqrt(down(cols[m], m))
            l = cols[m] * ri
            pivots = {}
            for i in range(m + 1, 8):
                pivots[i] = down(l, i)
                cols[i] = cols[i] - l * pivots[i]
            lm = jnp.where(sub > m, l, 0.0)
            u = down(p, m) * ri
            v = down(q, m) * ri
            p = jnp.where(sub == m, u, p - lm * u)
            q = jnp.where(sub == m, v, q - lm * v)
            rinv.append(ri)
            below.append(pivots)
            us.append(u)
            qs.append(v)
            if more:
                ln = cn[m] * ri
                for i in range(m + 1, 8):
                    cn[i] = cn[i] - ln * pivots[i]
                for i in range(8):
                    dn[i] = dn[i] - ln * down(ln, i)
                wn = wn - ln * u
                qn = qn - ln * v
        w_ref[here, :] = p
        q_ref[here, :] = q
        if more:
            w_ref[after, :] = wn
            q_ref[after, :] = qn
            cols = dn
        for t in range(k + 2, n):
            wt = w_ref[8 * t : 8 * t + 8, :]
            qt = q_ref[8 * t : 8 * t + 8, :]
            ct = [along(wt, 8 * k + m) for m in range(8)]
            for m in range(8):
                l = ct[m] * rinv[m]
                for i in range(m + 1, 8):
                    ct[i] = ct[i] - l * below[m][i]
                wt = wt - l * us[m]
                qt = qt - l * qs[m]
            w_ref[8 * t : 8 * t + 8, :] = wt
            q_ref[8 * t : 8 * t + 8, :] = qt


def sketch_kernel(nz, nx, scale, a_hbm, t_ref, basis_ref, out_ref, a_v, tg, part, rsr, s_ref, own, crecv, hb, prs, zr, fin, left, low, upper, diag, w_ref, q_ref, a_sem, zs, ys, ks, rs, cs, ps, gz, ag, ck):
    ny = NY
    r = lax.axis_index("row")
    x = lax.axis_index("col")
    c = lax.rem(r, NC)
    y = lax.rem(r // NC, ny)
    z = r // (NC * ny)
    ns = ny * nx
    s = y * nx + x
    share = s_ref.shape[0]

    def row_of(zz, yy, cc):
        return (zz * ny + yy) * NC + cc

    def z_peer(i):
        return (row_of(lax.rem(z + i, nz), y, c), x)

    nu = 2 * ns
    zb = lax.rem(z, 2)
    zp = z // 2
    nzp = nz // 2
    u = zb * ns + s

    def pair_peer(i):
        v = lax.rem(u + i, nu)
        q = lax.rem(v, ns)
        return v, (row_of(2 * zp + v // ns, q // nx, c), lax.rem(q, nx))

    def far_peer(i):
        return (row_of(2 * lax.rem(zp + i, nzp) + zb, y, c), x)

    sibling = (row_of(z, y, 1 - c), x)

    load_a = pltpu.make_async_copy(a_hbm, a_v, a_sem)
    load_a.start()
    barrier = pltpu.get_barrier_semaphore()

    def greet_z(i, carry):
        pl.semaphore_signal(barrier, inc=1, device_id=z_peer(i), device_id_type=MESH)
        return carry

    def greet_pair(i, carry):
        pl.semaphore_signal(barrier, inc=1, device_id=pair_peer(i)[1], device_id_type=MESH)
        return carry

    lax.fori_loop(1, nz, greet_z, 0)
    lax.fori_loop(1, nu, greet_pair, 0)
    pl.semaphore_signal(barrier, inc=1, device_id=sibling, device_id_type=MESH)
    for j in range(CHUNKS):
        tg[j, z, y, c] = t_ref[:, j * W : (j + 1) * W]
    pl.semaphore_wait(barrier, nz + nu - 1)

    def rcopy(src, dst, sems, k, to):
        return pltpu.make_async_remote_copy(
            src_ref=src, dst_ref=dst, send_sem=sems.at[0, k], recv_sem=sems.at[1, k],
            device_id=to, device_id_type=MESH,
        )

    def wait_bytes(view, sem):
        pltpu.make_async_copy(view, view, sem).wait()

    def z_send(j):
        def body(i, carry):
            rcopy(t_ref.at[:, pl.ds(j * W, W)], tg.at[j, z, y, c], zs, j, z_peer(i)).start()
            return carry
        lax.fori_loop(1, nz, body, 0)

    def z_view(j):
        return tg.at[j, pl.ds(0, nz - 1), y, c]

    def y_send(j):
        def body(i, carry):
            rcopy(tg.at[j, :, y, c], tg.at[j, :, y, c], ys, j, (row_of(z, lax.rem(y + i, ny), c), x)).start()
            return carry
        lax.fori_loop(1, ny, body, 0)

    def y_view(j):
        return tg.at[j, :, pl.ds(0, ny - 1), c]

    def k_copy(j):
        return rcopy(tg.at[j, :, :, c], tg.at[j, :, :, c], ks, j, sibling)

    def project(j):
        t_all = tg[j].reshape(-1, W)

        def block(d):
            q = lax.rem(x + d, nx)
            rows = pl.ds(pl.multiple_of(q * share, share), share)
            return q, jnp.dot(a_v[rows, :], t_all, preferred_element_type=jnp.float32)

        def body(i, carry):
            d = nx - 1 - i
            q, value = block(d)
            part[j, d] = value
            rcopy(part.at[j, d], rsr.at[j, d - 1], rs, j, (r, q)).start()
            return carry
        lax.fori_loop(0, nx - 1, body, 0)
        part[j, 0] = block(0)[1]

    def rs_view(j):
        return rsr.at[j]

    def finish_chunk(j):
        wait_bytes(rs_view(j), rs.at[1, j])
        total = part[j, 0]
        for d in range(nx - 1):
            total = total + rsr[j, d]
        s_ref[:, j * W : (j + 1) * W] = total

    def gram(g):
        n = (g + 1) * W
        value = lax.dot_general(
            s_ref[:, g * W : n], s_ref[:, 0:n], (((0,), (0,)), ((), ())),
            precision=HIGHEST, preferred_element_type=jnp.float32,
        )
        for i in range(g + 1):
            own[g, i // 2, i % 2] = value[:, i * W : (i + 1) * W]
        if g % 2 == 0:
            own[g, g // 2, 1] = jnp.zeros((W, W), jnp.float32)
        if g >= 2:
            rcopy(own.at[g, 1 - c], crecv.at[g - 2], cs, g - 2, sibling).start()

    def pair_send(g):
        if g >= 2:
            wait_bytes(crecv.at[g - 2], cs.at[1, g - 2])
            hb[g] = (own[g, c] + crecv[g - 2]).reshape(hb.shape[1:])
        else:
            hb[g] = own[g, 0].reshape(hb.shape[1:])

        def body(i, carry):
            v, to = pair_peer(i)
            rcopy(hb.at[g, v], prs.at[g, u], ps, g, to).start()
            return carry
        lax.fori_loop(1, nu, body, 0)
        prs[g, u] = hb[g, u]

    def pair_view(g):
        return prs.at[g, pl.ds(0, nu - 1)]

    def far_send(g):
        wait_bytes(pair_view(g), ps.at[1, g])
        zr[g, zp] = jnp.sum(prs[g], axis=0)

        def body(i, carry):
            rcopy(zr.at[g, zp], zr.at[g, zp], gz, g, far_peer(i)).start()
            return carry
        lax.fori_loop(1, nzp, body, 0)

    def far_view(g):
        return zr.at[g, pl.ds(0, nzp - 1)]

    def spread(g):
        wait_bytes(far_view(g), gz.at[1, g])
        fin[g, c, u] = jnp.sum(zr[g], axis=0)

        def body(i, carry):
            rcopy(fin.at[g, c, u], fin.at[g, c, u], ag, g, pair_peer(i)[1]).start()
            return carry
        lax.fori_loop(1, nu, body, 0)

    def spread_view(g):
        return fin.at[g, c, pl.ds(0, nu - 1)]

    def spread_core(g):
        wait_bytes(spread_view(g), ag.at[1, g])
        rcopy(fin.at[g, c], fin.at[g, c], ck, g, sibling).start()

    def spread_end(g):
        wait_bytes(fin.at[g, c], ck.at[1, g])

    row_at = lax.broadcasted_iota(jnp.int32, (W, W), 0)
    col_at = lax.broadcasted_iota(jnp.int32, (W, W), 1)
    done = []
    arrived = []

    def catch_up(j, b):
        l = mm(left[j, b], diag[b], 1, 1)
        low[j, b] = l
        for i in range(b + 1, j + 1):
            left[j, i] = left[j, i] - mm(l, low[i, b], 1, 1)

    def settle(j, b):
        l = low[j, b]
        upper[b, :, j * W : (j + 1) * W] = l.T
        block = (slice(None), slice(j * W, (j + 1) * W))
        basis_ref[block] = basis_ref[block] - mm(basis_ref[:, b * W : (b + 1) * W], l, 1, 1)

    def arrive(j):
        for i in range(j + 1):
            f, k = i // 2, slice((i % 2) * ns, (i % 2 + 1) * ns)
            tiles = fin[j, f, k] if j >= 2 else fin[j, 0, k] + fin[j, 1, k]
            left[j, i] = tiles.reshape(W, W) * scale
        basis_ref[:, j * W : (j + 1) * W] = s_ref[:, j * W : (j + 1) * W]
        arrived.append(j)
        for b in done:
            catch_up(j, b)
        for b in done:
            settle(j, b)

    def factor(b, hooks=None):
        w_ref[...] = left[b, b]
        factor_block(w_ref, q_ref, hooks)
        q = q_ref[...]
        diag[b] = q
        upper[b, :, b * W : (b + 1) * W] = jnp.where(col_at >= row_at, w_ref[...], 0.0)
        later = [j for j in arrived if j > b]
        for j in later:
            catch_up(j, b)
        block = (slice(None), slice(b * W, (b + 1) * W))
        basis_ref[block] = mm(basis_ref[block], q, 1, 1)
        for j in later:
            settle(j, b)
        done.append(b)

    for j in range(CHUNKS):
        z_send(j)

    def do_z(j):
        wait_bytes(z_view(j), zs.at[1, j])
        y_send(j)

    def do_y(j):
        wait_bytes(y_view(j), ys.at[1, j])
        k_copy(j).start()

    def do_k(j):
        wait_bytes(tg.at[j, :, :, c], ks.at[1, j])
        project(j)

    do_z(0)
    do_z(1)
    do_z(2)
    do_y(0)
    do_z(3)
    load_a.wait()
    do_k(0)
    do_y(1)
    do_k(1)
    do_y(2)
    do_k(2)
    do_y(3)
    do_k(3)
    finish_chunk(0)
    gram(0)
    pair_send(0)
    upper[...] = jnp.zeros_like(upper)
    finish_chunk(1)
    gram(1)
    pair_send(1)
    far_send(0)
    finish_chunk(2)
    gram(2)
    far_send(1)
    pair_send(2)
    spread(0)
    finish_chunk(3)
    gram(3)
    pair_send(3)
    far_send(2)
    spread(1)
    spread_core(0)
    spread_end(0)
    arrive(0)

    def early():
        far_send(3)

    def middle():
        spread_core(1)
        spread(2)

    factor(0, {2: early, 14: middle})
    spread_end(1)
    arrive(1)

    def third():
        spread_core(2)

    def fourth():
        spread(3)

    factor(1, {8: fourth, 13: third})
    spread_end(2)
    arrive(2)
    factor(2, {14: lambda: spread_core(3)})
    spread_end(3)
    arrive(3)
    factor(3)
    out_ref[...] = upper[x]

    for j in range(CHUNKS):
        wait_bytes(z_view(j), zs.at[0, j])
        wait_bytes(y_view(j), ys.at[0, j])
        wait_bytes(tg.at[j, :, :, c], ks.at[0, j])
        wait_bytes(rs_view(j), rs.at[0, j])
    for g in range(2):
        wait_bytes(crecv.at[g], cs.at[0, g])
    for g in range(CHUNKS):
        wait_bytes(pair_view(g), ps.at[0, g])
        wait_bytes(far_view(g), gz.at[0, g])
        wait_bytes(spread_view(g), ag.at[0, g])
        wait_bytes(fin.at[g, c], ck.at[0, g])


def solution(mesh):
    nx = mesh.shape["col"]
    nz = mesh.shape["row"] // (NY * NC)
    ns = NY * nx
    pr = W // ns
    f32 = jnp.float32
    dma = pltpu.SemaphoreType.DMA

    def on_device(travel_times, test_matrix):
        rows, cols = travel_times.shape
        depth, width = test_matrix.shape
        share = rows // nx
        scale = 1.0 / (rows * mesh.shape["row"])
        return pl.pallas_call(
            functools.partial(sketch_kernel, nz, nx, scale),
            out_shape=(
                jax.ShapeDtypeStruct((share, width), f32),
                jax.ShapeDtypeStruct((width // nx, width), f32),
            ),
            in_specs=[pl.BlockSpec(memory_space=pl.ANY), pl.BlockSpec(memory_space=pltpu.VMEM)],
            out_specs=[pl.BlockSpec(memory_space=pltpu.VMEM)] * 2,
            scratch_shapes=[
                pltpu.VMEM((rows, cols), jnp.bfloat16),
                pltpu.VMEM((CHUNKS, nz, NY, NC, depth, W), jnp.bfloat16),
                pltpu.VMEM((CHUNKS, nx, share, W), f32),
                pltpu.VMEM((CHUNKS, nx - 1, share, W), f32),
                pltpu.VMEM((share, width), f32),
                pltpu.VMEM((CHUNKS, 2, 2, W, W), f32),
                pltpu.VMEM((2, 2, W, W), f32),
                pltpu.VMEM((CHUNKS, 2 * ns, pr, W), f32),
                pltpu.VMEM((CHUNKS, 2 * ns, pr, W), f32),
                pltpu.VMEM((CHUNKS, nz // 2, pr, W), f32),
                pltpu.VMEM((CHUNKS, 2, 2 * ns, pr, W), f32),
                pltpu.VMEM((CHUNKS, CHUNKS, W, W), f32),
                pltpu.VMEM((CHUNKS, CHUNKS, W, W), f32),
                pltpu.VMEM((CHUNKS, W, width), f32),
                pltpu.VMEM((CHUNKS, W, W), f32),
                pltpu.VMEM((W, W), f32),
                pltpu.VMEM((W, W), f32),
                dma,
            ]
            + [dma((2, CHUNKS))] * 4
            + [dma((2, 2))]
            + [dma((2, CHUNKS))] * 4,
            compiler_params=pltpu.CompilerParams(
                collective_id=0, has_side_effects=True, vmem_limit_bytes=VMEM_MIB << 20
            ),
        )(travel_times, test_matrix)

    return jax.shard_map(
        on_device, mesh=mesh, in_specs=(P("row", "col"), P(("col", "row"), None)),
        out_specs=(P(("row", "col"), None), P("col", None)), check_vma=False,
    )
```

```python
import functools
import jax
import jax.numpy as jnp
from jax import lax
from jax.experimental import pallas as pl
from jax.experimental.pallas import tpu as pltpu
from jax.sharding import PartitionSpec as P

NY = 4
NC = 2
W = 128
CHUNKS = 4
VMEM_MIB = 58
MESH = pl.DeviceIdType.MESH


HIGHEST = lax.Precision.HIGHEST


def mm(a, b, ca, cb):
    return lax.dot_general(a, b, (((ca,), (cb,)), ((), ())), precision=HIGHEST, preferred_element_type=jnp.float32)


def factor_block(w_ref, q_ref, hooks=None):
    n = W // 8
    sub = lax.broadcasted_iota(jnp.int32, (8, W), 0)
    lane = lax.broadcasted_iota(jnp.int32, (8, W), 1)

    def along(v, i):
        return jnp.broadcast_to(v[:, i : i + 1], (8, W))

    def down(v, i):
        return jnp.broadcast_to(v[i : i + 1, :], (8, W))

    for t in range(n):
        q_ref[8 * t : 8 * t + 8, :] = jnp.where(lane == sub + 8 * t, 1.0, 0.0).astype(jnp.float32)
    first = w_ref[0:8, :]
    cols = [along(first, m) for m in range(8)]
    for k in range(n):
        if hooks and k in hooks:
            hooks[k]()
        here = slice(8 * k, 8 * k + 8)
        after = slice(8 * k + 8, 8 * k + 16)
        p = w_ref[here, :]
        q = q_ref[here, :]
        more = k + 1 < n
        if more:
            wn = w_ref[after, :]
            qn = q_ref[after, :]
            cn = [along(wn, 8 * k + m) for m in range(8)]
            dn = [along(wn, 8 * k + 8 + m) for m in range(8)]
        rinv, below, us, qs = [], [], [], []
        for m in range(8):
            ri = lax.rsqrt(down(cols[m], m))
            l = cols[m] * ri
            pivots = {}
            for i in range(m + 1, 8):
                pivots[i] = down(l, i)
                cols[i] = cols[i] - l * pivots[i]
            lm = jnp.where(sub > m, l, 0.0)
            u = down(p, m) * ri
            v = down(q, m) * ri
            p = jnp.where(sub == m, u, p - lm * u)
            q = jnp.where(sub == m, v, q - lm * v)
            rinv.append(ri)
            below.append(pivots)
            us.append(u)
            qs.append(v)
            if more:
                ln = cn[m] * ri
                for i in range(m + 1, 8):
                    cn[i] = cn[i] - ln * pivots[i]
                for i in range(8):
                    dn[i] = dn[i] - ln * down(ln, i)
                wn = wn - ln * u
                qn = qn - ln * v
        w_ref[here, :] = p
        q_ref[here, :] = q
        if more:
            w_ref[after, :] = wn
            q_ref[after, :] = qn
            cols = dn
        for t in range(k + 2, n):
            wt = w_ref[8 * t : 8 * t + 8, :]
            qt = q_ref[8 * t : 8 * t + 8, :]
            ct = [along(wt, 8 * k + m) for m in range(8)]
            for m in range(8):
                l = ct[m] * rinv[m]
                for i in range(m + 1, 8):
                    ct[i] = ct[i] - l * below[m][i]
                wt = wt - l * us[m]
                qt = qt - l * qs[m]
            w_ref[8 * t : 8 * t + 8, :] = wt
            q_ref[8 * t : 8 * t + 8, :] = qt


def sketch_kernel(nz, nx, scale, a_hbm, t_ref, basis_ref, out_ref, a_v, tg, part, rsr, s_ref, own, crecv, hb, prs, zr, fin, left, low, upper, diag, w_ref, q_ref, a_sem, zs, ys, ks, rq, rs, cs, ps, gz, ag, ck):
    ny = NY
    r = lax.axis_index("row")
    x = lax.axis_index("col")
    c = lax.rem(r, NC)
    y = lax.rem(r // NC, ny)
    z = r // (NC * ny)
    ns = ny * nx
    s = y * nx + x
    share = s_ref.shape[0]

    def row_of(zz, yy, cc):
        return (zz * ny + yy) * NC + cc

    def z_peer(i):
        return (row_of(lax.rem(z + i, nz), y, c), x)

    nu = 2 * ns
    zb = lax.rem(z, 2)
    zp = z // 2
    nzp = nz // 2
    u = zb * ns + s

    def pair_peer(i):
        v = lax.rem(u + i, nu)
        q = lax.rem(v, ns)
        return v, (row_of(2 * zp + v // ns, q // nx, c), lax.rem(q, nx))

    def far_peer(i):
        return (row_of(2 * lax.rem(zp + i, nzp) + zb, y, c), x)

    sibling = (row_of(z, y, 1 - c), x)

    load_a = pltpu.make_async_copy(a_hbm, a_v, a_sem)
    load_a.start()
    barrier = pltpu.get_barrier_semaphore()

    def greet_z(i, carry):
        pl.semaphore_signal(barrier, inc=1, device_id=z_peer(i), device_id_type=MESH)
        return carry

    def greet_pair(i, carry):
        pl.semaphore_signal(barrier, inc=1, device_id=pair_peer(i)[1], device_id_type=MESH)
        return carry

    lax.fori_loop(1, nz, greet_z, 0)
    lax.fori_loop(1, nu, greet_pair, 0)
    pl.semaphore_signal(barrier, inc=1, device_id=sibling, device_id_type=MESH)
    for j in range(CHUNKS):
        tg[j, z, y, c] = t_ref[:, j * W : (j + 1) * W]
    pl.semaphore_wait(barrier, nz + nu - 1)

    def rcopy(src, dst, sems, k, to):
        return pltpu.make_async_remote_copy(
            src_ref=src, dst_ref=dst, send_sem=sems.at[0, k], recv_sem=sems.at[1, k],
            device_id=to, device_id_type=MESH,
        )

    def wait_bytes(view, sem):
        pltpu.make_async_copy(view, view, sem).wait()

    def z_send(j):
        def body(i, carry):
            rcopy(t_ref.at[:, pl.ds(j * W, W)], tg.at[j, z, y, c], zs, j, z_peer(i)).start()
            return carry
        lax.fori_loop(1, nz, body, 0)

    def z_view(j):
        return tg.at[j, pl.ds(0, nz - 1), y, c]

    def y_send(j):
        def body(i, carry):
            rcopy(tg.at[j, :, y, c], tg.at[j, :, y, c], ys, j, (row_of(z, lax.rem(y + i, ny), c), x)).start()
            return carry
        lax.fori_loop(1, ny, body, 0)

    def y_view(j):
        return tg.at[j, :, pl.ds(0, ny - 1), c]

    def k_copy(j):
        return rcopy(tg.at[j, :, :, c], tg.at[j, :, :, c], ks, j, sibling)

    half_rows = share // 2
    top = pl.ds(0, half_rows)
    bottom = pl.ds(half_rows, half_rows)
    right = (r, lax.rem(x + 1, nx))
    left_dev = (r, lax.rem(x + nx - 1, nx))

    def project(j):
        t_all = tg[j].reshape(-1, W)

        def body(i, carry):
            d = lax.rem(i + 2, nx)
            q = lax.rem(x + d, nx)
            rows = pl.ds(pl.multiple_of(q * share, share), share)
            part[j, d] = jnp.dot(a_v[rows, :], t_all, preferred_element_type=jnp.float32)

            @pl.when(i == 0)
            def _():
                rcopy(part.at[j, 2, top], rsr.at[j, 0], rq, j, right).start()
                rcopy(part.at[j, 2, bottom], rsr.at[j, 1], rq, j, left_dev).start()

            @pl.when(i == 1)
            def _():
                rcopy(part.at[j, 3, top], rsr.at[j, 2], rs, j, left_dev).start()

            @pl.when(i == 3)
            def _():
                rcopy(part.at[j, 1, bottom], rsr.at[j, 3], rs, j, right).start()
            return carry
        lax.fori_loop(0, nx, body, 0)

    def relay(j):
        wait_bytes(relay_view(j), rq.at[1, j])
        part[j, 1, top] = part[j, 1, top] + rsr[j, 0]
        rcopy(part.at[j, 1, top], rsr.at[j, 4], rs, j, right).start()
        part[j, 3, bottom] = part[j, 3, bottom] + rsr[j, 1]
        rcopy(part.at[j, 3, bottom], rsr.at[j, 5], rs, j, left_dev).start()

    def relay_view(j):
        return rsr.at[j, pl.ds(0, 2)]

    def rs_view(j):
        return rsr.at[j, pl.ds(2, 4)]

    def finish_chunk(j):
        wait_bytes(rs_view(j), rs.at[1, j])
        cols = slice(j * W, (j + 1) * W)
        s_ref[:half_rows, cols] = (part[j, 0, top] + rsr[j, 2]) + rsr[j, 4]
        s_ref[half_rows:, cols] = (part[j, 0, bottom] + rsr[j, 3]) + rsr[j, 5]

    def gram(g):
        start = 0 if g == 0 else (g + 1) * W
        n = (g + 2) * W
        value = lax.dot_general(
            s_ref[:, start:n], s_ref[:, 0:n], (((0,), (0,)), ((), ())),
            precision=HIGHEST, preferred_element_type=jnp.float32,
        )
        for half in range(2):
            for k in range(2):
                i, j = (half, k) if g == 0 else (0, 2 * half + k)
                if j <= (i if g == 0 else g + 1):
                    own[g, half, k] = value[i * W : (i + 1) * W, j * W : (j + 1) * W]
                else:
                    own[g, half, k] = jnp.zeros((W, W), jnp.float32)
        rcopy(own.at[g, 1 - c], crecv.at[g], cs, g, sibling).start()

    def pair_send(g):
        wait_bytes(crecv.at[g], cs.at[1, g])
        hb[g] = (own[g, c] + crecv[g]).reshape(hb.shape[1:])

        def body(i, carry):
            v, to = pair_peer(i)
            rcopy(hb.at[g, v], prs.at[g, u], ps, g, to).start()
            return carry
        lax.fori_loop(1, nu, body, 0)
        prs[g, u] = hb[g, u]

    def pair_view(g):
        return prs.at[g, pl.ds(0, nu - 1)]

    def far_send(g):
        wait_bytes(pair_view(g), ps.at[1, g])
        zr[g, zp] = jnp.sum(prs[g], axis=0)

        def body(i, carry):
            rcopy(zr.at[g, zp], zr.at[g, zp], gz, g, far_peer(i)).start()
            return carry
        lax.fori_loop(1, nzp, body, 0)

    def far_view(g):
        return zr.at[g, pl.ds(0, nzp - 1)]

    def spread(g):
        wait_bytes(far_view(g), gz.at[1, g])
        fin[g, c, u] = jnp.sum(zr[g], axis=0)

        def body(i, carry):
            rcopy(fin.at[g, c, u], fin.at[g, c, u], ag, g, pair_peer(i)[1]).start()
            return carry
        lax.fori_loop(1, nu, body, 0)

    def spread_view(g):
        return fin.at[g, c, pl.ds(0, nu - 1)]

    def spread_core(g):
        wait_bytes(spread_view(g), ag.at[1, g])
        rcopy(fin.at[g, c], fin.at[g, c], ck, g, sibling).start()

    def spread_end(g):
        wait_bytes(fin.at[g, c], ck.at[1, g])

    row_at = lax.broadcasted_iota(jnp.int32, (W, W), 0)
    col_at = lax.broadcasted_iota(jnp.int32, (W, W), 1)
    done = []
    arrived = []

    def catch_up(j, b):
        l = mm(left[j, b], diag[b], 1, 1)
        low[j, b] = l
        for i in range(b + 1, j + 1):
            left[j, i] = left[j, i] - mm(l, low[i, b], 1, 1)

    def settle(j, b):
        l = low[j, b]
        upper[b, :, j * W : (j + 1) * W] = l.T
        block = (slice(None), slice(j * W, (j + 1) * W))
        basis_ref[block] = basis_ref[block] - mm(basis_ref[:, b * W : (b + 1) * W], l, 1, 1)

    def arrive(j):
        g = max(j - 1, 0)
        for i in range(j + 1):
            f, k = (j, i) if j < 2 else (i // 2, i % 2)
            left[j, i] = fin[g, f, k * ns : (k + 1) * ns].reshape(W, W) * scale
        basis_ref[:, j * W : (j + 1) * W] = s_ref[:, j * W : (j + 1) * W]
        arrived.append(j)
        for b in done:
            catch_up(j, b)
        for b in done:
            settle(j, b)

    def factor(b, hooks=None):
        w_ref[...] = left[b, b]
        factor_block(w_ref, q_ref, hooks)
        q = q_ref[...]
        diag[b] = q
        upper[b, :, b * W : (b + 1) * W] = jnp.where(col_at >= row_at, w_ref[...], 0.0)
        later = [j for j in arrived if j > b]
        for j in later:
            catch_up(j, b)
        block = (slice(None), slice(b * W, (b + 1) * W))
        basis_ref[block] = mm(basis_ref[block], q, 1, 1)
        for j in later:
            settle(j, b)
        done.append(b)

    for j in range(CHUNKS):
        z_send(j)

    def do_z(j):
        wait_bytes(z_view(j), zs.at[1, j])
        y_send(j)

    def do_y(j):
        wait_bytes(y_view(j), ys.at[1, j])
        k_copy(j).start()

    def do_k(j):
        wait_bytes(tg.at[j, :, :, c], ks.at[1, j])
        project(j)

    do_z(0)
    do_z(1)
    do_z(2)
    do_y(0)
    do_z(3)
    load_a.wait()
    do_k(0)
    do_y(1)
    do_k(1)
    do_y(2)
    relay(0)
    do_k(2)
    do_y(3)
    relay(1)
    do_k(3)
    relay(2)
    finish_chunk(0)
    upper[...] = jnp.zeros_like(upper)
    relay(3)
    finish_chunk(1)
    gram(0)
    pair_send(0)
    finish_chunk(2)
    gram(1)
    pair_send(1)
    finish_chunk(3)
    gram(2)
    far_send(0)
    pair_send(2)
    far_send(1)
    far_send(2)
    spread(0)
    spread(1)
    spread_core(0)
    spread_end(0)
    spread(2)
    arrive(0)
    arrive(1)
    factor(0)
    spread_core(1)
    factor(1)
    spread_end(1)
    spread_core(2)
    arrive(2)
    factor(2)
    spread_end(2)
    arrive(3)
    factor(3)
    out_ref[...] = upper[x]

    for j in range(CHUNKS):
        wait_bytes(z_view(j), zs.at[0, j])
        wait_bytes(y_view(j), ys.at[0, j])
        wait_bytes(tg.at[j, :, :, c], ks.at[0, j])
        wait_bytes(relay_view(j), rq.at[0, j])
        wait_bytes(rs_view(j), rs.at[0, j])
    for g in range(3):
        wait_bytes(crecv.at[g], cs.at[0, g])
        wait_bytes(pair_view(g), ps.at[0, g])
        wait_bytes(far_view(g), gz.at[0, g])
        wait_bytes(spread_view(g), ag.at[0, g])
        wait_bytes(fin.at[g, c], ck.at[0, g])


def solution(mesh):
    nx = mesh.shape["col"]
    nz = mesh.shape["row"] // (NY * NC)
    ns = NY * nx
    pr = W // ns
    f32 = jnp.float32
    dma = pltpu.SemaphoreType.DMA

    def on_device(travel_times, test_matrix):
        rows, cols = travel_times.shape
        depth, width = test_matrix.shape
        share = rows // nx
        scale = 1.0 / (rows * mesh.shape["row"])
        return pl.pallas_call(
            functools.partial(sketch_kernel, nz, nx, scale),
            out_shape=(
                jax.ShapeDtypeStruct((share, width), f32),
                jax.ShapeDtypeStruct((width // nx, width), f32),
            ),
            in_specs=[pl.BlockSpec(memory_space=pl.ANY), pl.BlockSpec(memory_space=pltpu.VMEM)],
            out_specs=[pl.BlockSpec(memory_space=pltpu.VMEM)] * 2,
            scratch_shapes=[
                pltpu.VMEM((rows, cols), jnp.bfloat16),
                pltpu.VMEM((CHUNKS, nz, NY, NC, depth, W), jnp.bfloat16),
                pltpu.VMEM((CHUNKS, nx, share, W), f32),
                pltpu.VMEM((CHUNKS, 6, share // 2, W), f32),
                pltpu.VMEM((share, width), f32),
                pltpu.VMEM((3, 2, 2, W, W), f32),
                pltpu.VMEM((3, 2, W, W), f32),
                pltpu.VMEM((3, 2 * ns, pr, W), f32),
                pltpu.VMEM((3, 2 * ns, pr, W), f32),
                pltpu.VMEM((3, nz // 2, pr, W), f32),
                pltpu.VMEM((3, 2, 2 * ns, pr, W), f32),
                pltpu.VMEM((CHUNKS, CHUNKS, W, W), f32),
                pltpu.VMEM((CHUNKS, CHUNKS, W, W), f32),
                pltpu.VMEM((CHUNKS, W, width), f32),
                pltpu.VMEM((CHUNKS, W, W), f32),
                pltpu.VMEM((W, W), f32),
                pltpu.VMEM((W, W), f32),
                dma,
            ]
            + [dma((2, CHUNKS))] * 5
            + [dma((2, 3))] * 5,
            compiler_params=pltpu.CompilerParams(
                collective_id=0, has_side_effects=True, vmem_limit_bytes=VMEM_MIB << 20
            ),
        )(travel_times, test_matrix)

    return jax.shard_map(
        on_device, mesh=mesh, in_specs=(P("row", "col"), P(("col", "row"), None)),
        out_specs=(P(("row", "col"), None), P("col", None)), check_vma=False,
    )
```

```python
import functools
import jax
import jax.numpy as jnp
from jax import lax
from jax.experimental import pallas as pl
from jax.experimental.pallas import tpu as pltpu
from jax.sharding import PartitionSpec as P

NY = 4
NC = 2
W = 128
CHUNKS = 4
VMEM_MIB = 52
MESH = pl.DeviceIdType.MESH


HIGHEST = lax.Precision.HIGHEST


def mm(a, b, ca, cb):
    return lax.dot_general(a, b, (((ca,), (cb,)), ((), ())), precision=HIGHEST, preferred_element_type=jnp.float32)


def factor_block(w_ref, q_ref, hooks=None):
    n = W // 8
    sub = lax.broadcasted_iota(jnp.int32, (8, W), 0)
    lane = lax.broadcasted_iota(jnp.int32, (8, W), 1)

    def along(v, i):
        return jnp.broadcast_to(v[:, i : i + 1], (8, W))

    def down(v, i):
        return jnp.broadcast_to(v[i : i + 1, :], (8, W))

    for t in range(n):
        q_ref[8 * t : 8 * t + 8, :] = jnp.where(lane == sub + 8 * t, 1.0, 0.0).astype(jnp.float32)
    first = w_ref[0:8, :]
    cols = [along(first, m) for m in range(8)]
    for k in range(n):
        if hooks and k in hooks:
            hooks[k]()
        here = slice(8 * k, 8 * k + 8)
        after = slice(8 * k + 8, 8 * k + 16)
        p = w_ref[here, :]
        q = q_ref[here, :]
        more = k + 1 < n
        if more:
            wn = w_ref[after, :]
            qn = q_ref[after, :]
            cn = [along(wn, 8 * k + m) for m in range(8)]
            dn = [along(wn, 8 * k + 8 + m) for m in range(8)]
        rinv, below, us, qs = [], [], [], []
        for m in range(8):
            ri = lax.rsqrt(down(cols[m], m))
            l = cols[m] * ri
            pivots = {}
            for i in range(m + 1, 8):
                pivots[i] = down(l, i)
                cols[i] = cols[i] - l * pivots[i]
            lm = jnp.where(sub > m, l, 0.0)
            u = down(p, m) * ri
            v = down(q, m) * ri
            p = jnp.where(sub == m, u, p - lm * u)
            q = jnp.where(sub == m, v, q - lm * v)
            rinv.append(ri)
            below.append(pivots)
            us.append(u)
            qs.append(v)
            if more:
                ln = cn[m] * ri
                for i in range(m + 1, 8):
                    cn[i] = cn[i] - ln * pivots[i]
                for i in range(8):
                    dn[i] = dn[i] - ln * down(ln, i)
                wn = wn - ln * u
                qn = qn - ln * v
        w_ref[here, :] = p
        q_ref[here, :] = q
        if more:
            w_ref[after, :] = wn
            q_ref[after, :] = qn
            cols = dn
        for t in range(k + 2, n):
            wt = w_ref[8 * t : 8 * t + 8, :]
            qt = q_ref[8 * t : 8 * t + 8, :]
            ct = [along(wt, 8 * k + m) for m in range(8)]
            for m in range(8):
                l = ct[m] * rinv[m]
                for i in range(m + 1, 8):
                    ct[i] = ct[i] - l * below[m][i]
                wt = wt - l * us[m]
                qt = qt - l * qs[m]
            w_ref[8 * t : 8 * t + 8, :] = wt
            q_ref[8 * t : 8 * t + 8, :] = qt


def sketch_kernel(nz, nx, scale, a_hbm, t_ref, basis_ref, out_ref, a_v, tg, part, rsr, s_ref, own, crecv, hb, prs, zr, fin, left, low, upper, diag, w_ref, q_ref, a_sem, zs, ys, ks, rq, rs, cs, ps, gz, ag, ck):
    ny = NY
    r = lax.axis_index("row")
    x = lax.axis_index("col")
    c = lax.rem(r, NC)
    y = lax.rem(r // NC, ny)
    z = r // (NC * ny)
    ns = ny * nx
    s = y * nx + x
    share = s_ref.shape[0]

    def row_of(zz, yy, cc):
        return (zz * ny + yy) * NC + cc

    def z_peer(i):
        return (row_of(lax.rem(z + i, nz), y, c), x)

    nu = 2 * ns
    zb = lax.rem(z, 2)
    zp = z // 2
    nzp = nz // 2
    u = zb * ns + s

    def pair_peer(i):
        v = lax.rem(u + i, nu)
        q = lax.rem(v, ns)
        return v, (row_of(2 * zp + v // ns, q // nx, c), lax.rem(q, nx))

    def far_peer(i):
        return (row_of(2 * lax.rem(zp + i, nzp) + zb, y, c), x)

    sibling = (row_of(z, y, 1 - c), x)

    load_a = pltpu.make_async_copy(a_hbm, a_v, a_sem)
    load_a.start()
    barrier = pltpu.get_barrier_semaphore()

    def greet_z(i, carry):
        pl.semaphore_signal(barrier, inc=1, device_id=z_peer(i), device_id_type=MESH)
        return carry

    def greet_pair(i, carry):
        pl.semaphore_signal(barrier, inc=1, device_id=pair_peer(i)[1], device_id_type=MESH)
        return carry

    lax.fori_loop(1, nz, greet_z, 0)
    lax.fori_loop(1, nu, greet_pair, 0)
    pl.semaphore_signal(barrier, inc=1, device_id=sibling, device_id_type=MESH)
    for j in range(CHUNKS):
        tg[j, z, y, c] = t_ref[:, j * W : (j + 1) * W]
    pl.semaphore_wait(barrier, nz + nu - 1)

    def rcopy(src, dst, sems, k, to):
        return pltpu.make_async_remote_copy(
            src_ref=src, dst_ref=dst, send_sem=sems.at[0, k], recv_sem=sems.at[1, k],
            device_id=to, device_id_type=MESH,
        )

    def wait_bytes(view, sem):
        pltpu.make_async_copy(view, view, sem).wait()

    def z_send(j):
        def body(i, carry):
            rcopy(t_ref.at[:, pl.ds(j * W, W)], tg.at[j, z, y, c], zs, j, z_peer(i)).start()
            return carry
        lax.fori_loop(1, nz, body, 0)

    def z_view(j):
        return tg.at[j, pl.ds(0, nz - 1), y, c]

    def y_send(j):
        def body(i, carry):
            rcopy(tg.at[j, :, y, c], tg.at[j, :, y, c], ys, j, (row_of(z, lax.rem(y + i, ny), c), x)).start()
            return carry
        lax.fori_loop(1, ny, body, 0)

    def y_view(j):
        return tg.at[j, :, pl.ds(0, ny - 1), c]

    def k_copy(j):
        return rcopy(tg.at[j, :, :, c], tg.at[j, :, :, c], ks, j, sibling)

    half_rows = share // 2
    top = pl.ds(0, half_rows)
    bottom = pl.ds(half_rows, half_rows)
    right = (r, lax.rem(x + 1, nx))
    left_dev = (r, lax.rem(x + nx - 1, nx))

    def project(j):
        t_all = tg[j].reshape(-1, W)

        def body(i, carry):
            d = lax.rem(i + 2, nx)
            q = lax.rem(x + d, nx)
            rows = pl.ds(pl.multiple_of(q * share, share), share)
            part[j, d] = jnp.dot(a_v[rows, :], t_all, preferred_element_type=jnp.float32)

            @pl.when(i == 0)
            def _():
                rcopy(part.at[j, 2, top], rsr.at[j, 0], rq, j, right).start()
                rcopy(part.at[j, 2, bottom], rsr.at[j, 1], rq, j, left_dev).start()

            @pl.when(i == 1)
            def _():
                rcopy(part.at[j, 3, top], rsr.at[j, 2], rs, j, left_dev).start()

            @pl.when(i == 3)
            def _():
                rcopy(part.at[j, 1, bottom], rsr.at[j, 3], rs, j, right).start()
            return carry
        lax.fori_loop(0, nx, body, 0)

    def relay(j):
        wait_bytes(relay_view(j), rq.at[1, j])
        part[j, 1, top] = part[j, 1, top] + rsr[j, 0]
        rcopy(part.at[j, 1, top], rsr.at[j, 4], rs, j, right).start()
        part[j, 3, bottom] = part[j, 3, bottom] + rsr[j, 1]
        rcopy(part.at[j, 3, bottom], rsr.at[j, 5], rs, j, left_dev).start()

    def relay_view(j):
        return rsr.at[j, pl.ds(0, 2)]

    def rs_view(j):
        return rsr.at[j, pl.ds(2, 4)]

    def finish_chunk(j):
        wait_bytes(rs_view(j), rs.at[1, j])
        cols = slice(j * W, (j + 1) * W)
        s_ref[:half_rows, cols] = (part[j, 0, top] + rsr[j, 2]) + rsr[j, 4]
        s_ref[half_rows:, cols] = (part[j, 0, bottom] + rsr[j, 3]) + rsr[j, 5]

    def gram(g):
        start = 0 if g == 0 else (g + 1) * W
        n = (g + 2) * W
        value = lax.dot_general(
            s_ref[:, start:n], s_ref[:, 0:n], (((0,), (0,)), ((), ())),
            precision=HIGHEST, preferred_element_type=jnp.float32,
        )
        for half in range(2):
            for k in range(2):
                i, j = (half, k) if g == 0 else (0, 2 * half + k)
                if j <= (i if g == 0 else g + 1):
                    own[g, half, k] = value[i * W : (i + 1) * W, j * W : (j + 1) * W]
                else:
                    own[g, half, k] = jnp.zeros((W, W), jnp.float32)
        rcopy(own.at[g, 1 - c], crecv.at[g], cs, g, sibling).start()

    def pair_send(g):
        wait_bytes(crecv.at[g], cs.at[1, g])
        hb[g] = (own[g, c] + crecv[g]).reshape(hb.shape[1:])

        def body(i, carry):
            v, to = pair_peer(i)
            rcopy(hb.at[g, v], prs.at[g, u], ps, g, to).start()
            return carry
        lax.fori_loop(1, nu, body, 0)
        prs[g, u] = hb[g, u]

    def pair_view(g):
        return prs.at[g, pl.ds(0, nu - 1)]

    def far_send(g):
        wait_bytes(pair_view(g), ps.at[1, g])
        zr[g, zp] = jnp.sum(prs[g], axis=0)

        def body(i, carry):
            rcopy(zr.at[g, zp], zr.at[g, zp], gz, g, far_peer(i)).start()
            return carry
        lax.fori_loop(1, nzp, body, 0)

    def far_view(g):
        return zr.at[g, pl.ds(0, nzp - 1)]

    def spread(g):
        wait_bytes(far_view(g), gz.at[1, g])
        fin[g, c, u] = jnp.sum(zr[g], axis=0)

        def body(i, carry):
            rcopy(fin.at[g, c, u], fin.at[g, c, u], ag, g, pair_peer(i)[1]).start()
            return carry
        lax.fori_loop(1, nu, body, 0)

    def spread_view(g):
        return fin.at[g, c, pl.ds(0, nu - 1)]

    def spread_core(g):
        wait_bytes(spread_view(g), ag.at[1, g])
        rcopy(fin.at[g, c], fin.at[g, c], ck, g, sibling).start()

    def spread_end(g):
        wait_bytes(fin.at[g, c], ck.at[1, g])

    row_at = lax.broadcasted_iota(jnp.int32, (W, W), 0)
    col_at = lax.broadcasted_iota(jnp.int32, (W, W), 1)

    def catch_up(j, b):
        l = mm(left[j, b], diag[b], 1, 1)
        low[j, b] = l
        for i in range(b + 1, j + 1):
            left[j, i] = left[j, i] - mm(l, low[i, b], 1, 1)

    def arrive(j, factored):
        g = max(j - 1, 0)
        for i in range(j + 1):
            f, k = (j, i) if j < 2 else (i // 2, i % 2)
            left[j, i] = fin[g, f, k * ns : (k + 1) * ns].reshape(W, W) * scale
        for b in range(factored):
            catch_up(j, b)

    def basis(b):
        here = slice(b * W, (b + 1) * W)
        value = s_ref[:, here]
        for m in range(b):
            value = value - mm(basis_ref[:, m * W : (m + 1) * W], low[b, m], 1, 1)
            upper[m, :, here] = low[b, m].T
        basis_ref[:, here] = value if b == CHUNKS - 1 else mm(value, diag[b], 1, 1)

    def factor(b, hooks=None):
        w_ref[...] = left[b, b]
        factor_block(w_ref, q_ref, hooks)
        diag[b] = q_ref[...]
        upper[b, :, b * W : (b + 1) * W] = jnp.where(col_at >= row_at, w_ref[...], 0.0)

    for j in range(CHUNKS):
        z_send(j)

    def do_z(j):
        wait_bytes(z_view(j), zs.at[1, j])
        y_send(j)

    def do_y(j):
        wait_bytes(y_view(j), ys.at[1, j])
        k_copy(j).start()

    def do_k(j):
        wait_bytes(tg.at[j, :, :, c], ks.at[1, j])
        project(j)

    do_z(0)
    do_z(1)
    do_z(2)
    do_y(0)
    do_z(3)
    load_a.wait()
    do_k(0)
    do_y(1)
    do_k(1)
    do_y(2)
    relay(0)
    do_k(2)
    do_y(3)
    relay(1)
    do_k(3)
    relay(2)
    finish_chunk(0)
    upper[...] = jnp.zeros_like(upper)
    relay(3)
    finish_chunk(1)
    gram(0)
    pair_send(0)
    finish_chunk(2)
    gram(1)
    pair_send(1)
    finish_chunk(3)
    gram(2)
    far_send(0)
    pair_send(2)
    far_send(1)
    far_send(2)
    spread(0)
    spread(1)
    spread_core(0)
    spread_end(0)
    arrive(0, 0)
    arrive(1, 0)
    factor(0, {3: lambda: spread(2), 13: lambda: spread_core(1)})
    catch_up(1, 0)

    def row_two():
        spread_end(1)
        arrive(2, 1)

    def row_three():
        spread_end(2)
        arrive(3, 2)

    factor(1, {2: lambda: basis(0), 6: row_two, 12: lambda: spread_core(2)})
    catch_up(2, 1)
    factor(2, {2: lambda: basis(1), 6: row_three})
    catch_up(3, 2)
    factor(3, {2: lambda: basis(2), 6: lambda: basis(3)})
    last = slice((CHUNKS - 1) * W, CHUNKS * W)
    basis_ref[:, last] = mm(basis_ref[:, last], diag[CHUNKS - 1], 1, 1)
    out_ref[...] = upper[x]

    for j in range(CHUNKS):
        wait_bytes(z_view(j), zs.at[0, j])
        wait_bytes(y_view(j), ys.at[0, j])
        wait_bytes(tg.at[j, :, :, c], ks.at[0, j])
        wait_bytes(relay_view(j), rq.at[0, j])
        wait_bytes(rs_view(j), rs.at[0, j])
    for g in range(3):
        wait_bytes(crecv.at[g], cs.at[0, g])
        wait_bytes(pair_view(g), ps.at[0, g])
        wait_bytes(far_view(g), gz.at[0, g])
        wait_bytes(spread_view(g), ag.at[0, g])
        wait_bytes(fin.at[g, c], ck.at[0, g])


def solution(mesh):
    nx = mesh.shape["col"]
    nz = mesh.shape["row"] // (NY * NC)
    ns = NY * nx
    pr = W // ns
    f32 = jnp.float32
    dma = pltpu.SemaphoreType.DMA

    def on_device(travel_times, test_matrix):
        rows, cols = travel_times.shape
        depth, width = test_matrix.shape
        share = rows // nx
        scale = 1.0 / (rows * mesh.shape["row"])
        return pl.pallas_call(
            functools.partial(sketch_kernel, nz, nx, scale),
            out_shape=(
                jax.ShapeDtypeStruct((share, width), f32),
                jax.ShapeDtypeStruct((width // nx, width), f32),
            ),
            in_specs=[pl.BlockSpec(memory_space=pl.ANY), pl.BlockSpec(memory_space=pltpu.VMEM)],
            out_specs=[pl.BlockSpec(memory_space=pltpu.VMEM)] * 2,
            scratch_shapes=[
                pltpu.VMEM((rows, cols), jnp.bfloat16),
                pltpu.VMEM((CHUNKS, nz, NY, NC, depth, W), jnp.bfloat16),
                pltpu.VMEM((CHUNKS, nx, share, W), f32),
                pltpu.VMEM((CHUNKS, 6, share // 2, W), f32),
                pltpu.VMEM((share, width), f32),
                pltpu.VMEM((3, 2, 2, W, W), f32),
                pltpu.VMEM((3, 2, W, W), f32),
                pltpu.VMEM((3, 2 * ns, pr, W), f32),
                pltpu.VMEM((3, 2 * ns, pr, W), f32),
                pltpu.VMEM((3, nz // 2, pr, W), f32),
                pltpu.VMEM((3, 2, 2 * ns, pr, W), f32),
                pltpu.VMEM((CHUNKS, CHUNKS, W, W), f32),
                pltpu.VMEM((CHUNKS, CHUNKS, W, W), f32),
                pltpu.VMEM((CHUNKS, W, width), f32),
                pltpu.VMEM((CHUNKS, W, W), f32),
                pltpu.VMEM((W, W), f32),
                pltpu.VMEM((W, W), f32),
                dma,
            ]
            + [dma((2, CHUNKS))] * 5
            + [dma((2, 3))] * 5,
            compiler_params=pltpu.CompilerParams(
                collective_id=0, has_side_effects=True, vmem_limit_bytes=VMEM_MIB << 20
            ),
        )(travel_times, test_matrix)

    return jax.shard_map(
        on_device, mesh=mesh, in_specs=(P("row", "col"), P(("col", "row"), None)),
        out_specs=(P(("row", "col"), None), P("col", None)), check_vma=False,
    )
```
